32 devices in a mesh: dom: 8 (over z, x), neu: 4 (over y, core).
Axes of the slice: x: 2, y: 2, z: 4, core: 2. Of those that a mesh axis runs over, the one named last changes fastest.
Arguments:
- state_lower: bfloat16 [2, 3072, 8192], P(None, 'dom', 'neu'), may hold values from -4 to 4
- state_gap: bfloat16 [2, 3072, 8192], P(None, 'dom', 'neu'), may hold values from 0.099609375 to 4
- state_alpha: bfloat16 [2, 3072, 2, 8192], P(None, 'dom', None, 'neu'), may hold values from 0 to 1
- split_beta: bfloat16 [3072, 2], P('dom'), may hold values from 0.0019989014 to 0.029907227
- split_neuron: int32 [3072], P('dom'), may hold values from 0 to 16383
- split_sign: int32 [3072], P('dom'), may hold values 0 or 1
- send_counts: int32 [8, 8], replicated, may hold values from 0 to 48, as said below
- spec_row: bfloat16 [8192], P('neu'), may hold values from -0.0007324219 to 0.0007324219
- weight: bfloat16 [8192, 8192], P('neu', 'dom'), may hold values from -0.09375 to 0.09375
Outputs:
- moved_lower: bfloat16 [2, 1536, 8192], P(None, 'dom', 'neu')
- moved_gap: bfloat16 [2, 1536, 8192], P(None, 'dom', 'neu')
- moved_alpha: bfloat16 [2, 1536, 2, 8192], P(None, 'dom', None, 'neu')
- moved_beta: bfloat16 [1536, 2], P('dom')
- moved_neuron: int32 [1536], P('dom')
- moved_sign: int32 [1536], P('dom')
- bounds: float32 [1536, 2], P('dom')
The draws below stay inside these ranges and needn't reach their ends.
Inputs may be any that keep to these rules, and one draw needn't show every extreme that they name: send_counts[d, e] subdomains go from device d to device e of dom; every column sums to 192; the devices fall into pairs, drawn from the seed, whose two counts to any destination add up to 48; some entry equals 48.
All inputs are finite; a program needn't handle non-finite values. No bound on the sum of `split_sign` on one device may be relied on, other than what follows from the above.
Results may differ from the reference program's by a relative error of at most 0.001.
Values may be sent and summed in bfloat16 or wider, within the bound.
No kernel may reach another device: no remote copies, remote signals or barrier semaphores. Data moves between devices by JAX's collectives and lax.ppermute only.
A program may use at most 192 MiB of HBM per device.

```python
import math
import jax
import jax.numpy as jnp

WIDTH = 8192
RELU_LAYERS = 2
DOM_DEV = 192
CAP = 48
SLOTS = 3072
N_DOM = 8


def draw_send_counts(key, part):
    key_pair = jax.random.fold_in(key, 11)
    key_bias = jax.random.fold_in(key, 12)
    key_jitter = jax.random.fold_in(key, 13)
    key_full = jax.random.fold_in(key, 14)
    pairing = jax.random.permutation(key_pair, N_DOM).astype(jnp.int32)
    bias_draw = jax.random.randint(key_bias, (N_DOM // 2, 1), 0, CAP + 1)
    jitter = jax.random.randint(key_jitter, (N_DOM // 2, N_DOM), -(CAP // 4), CAP // 4 + 1)
    first_half = jnp.clip(bias_draw + jitter, 0, CAP)
    full_column = jax.random.randint(key_full, (), 0, N_DOM)
    first_half = first_half.at[0, full_column].set(CAP)
    second = CAP - first_half
    counts = jnp.zeros((N_DOM, N_DOM), jnp.int32)
    counts = counts.at[pairing[0::2]].set(first_half).at[pairing[1::2]].set(second)
    return counts.astype(jnp.int32)


def set_ends(values, key, smallest, top_value):
    spot = [jax.random.randint(jax.random.fold_in(key, axis), (), 0, length) for axis, length in enumerate(values.shape)]
    longest = values.shape.index(max(values.shape))
    beside = spot[:longest] + [(spot[longest] + 1) % values.shape[longest]] + spot[longest + 1:]
    return values.at[tuple(spot)].set(smallest).at[tuple(beside)].set(top_value)


def spiked(values, key, source, target, blocks, factor):
    def block_of(axis_at):
        return (jnp.arange(values.shape[axis_at]) // (values.shape[axis_at] // blocks)).reshape((-1,) + (1,) * (values.ndim - 1 - axis_at))

    first = jax.random.permutation(key, blocks)[block_of(target)]
    far = (block_of(target) + blocks // 2) % blocks
    return jnp.where((block_of(source) == first) | (block_of(source) == far), factor * values, values)


def levels(rng, shape, cuts, low, top_value):
    factor_of, own = 1.0, jax.random.fold_in(rng, 6)
    for position, blocks in cuts:
        heights = jnp.exp(jax.random.uniform(jax.random.fold_in(own, position), (blocks,), jnp.float32, low / len(cuts), top_value / len(cuts)))
        factor_of = factor_of * jnp.repeat(heights, shape[position] // blocks).reshape([-1 if axis == position else 1 for axis in range(len(shape))])
    return factor_of


def bell_draw(rng, dims, width, bound, shards=(), kind=jnp.bfloat16):
    values = width * jax.random.normal(rng, dims, jnp.float32)
    if shards:
        values = values * levels(rng, dims, shards, -0.22, 0.18)
    return jnp.clip(values, -bound, bound).astype(kind)


def heavy_noise(rng, extent, spread, most, split, heavy, held_as=jnp.bfloat16):
    values = spread * jax.random.normal(rng, extent, jnp.float32)
    if split:
        values = values * levels(rng, extent, split, -0.22, 0.18)
    return jnp.clip(spiked(values, jax.random.fold_in(rng, 3), *heavy), -most, most).astype(held_as)


def setup_inputs(seed: int = 0) -> dict:
    arg_keys = jax.random.split(jax.random.key(seed), 10)
    return {
        "state_lower": bell_draw(arg_keys[0], (RELU_LAYERS, SLOTS, WIDTH), 1.0, 4.0, ((1, 8), (2, 4))),
        "state_gap": jnp.clip(jnp.exp(math.log(4.0) - 3.6927934 * jax.random.uniform(arg_keys[1], (RELU_LAYERS, SLOTS, WIDTH), jnp.float32) ** levels(arg_keys[1], (RELU_LAYERS, SLOTS, WIDTH), ((1, 8), (2, 4)), -0.2, 0.2)), 0.099609375, 4.0).astype(jnp.bfloat16),
        "state_alpha": jnp.clip(1.0 * jax.random.uniform(arg_keys[2], (RELU_LAYERS, SLOTS, 2, WIDTH), jnp.float32) ** levels(arg_keys[2], (RELU_LAYERS, SLOTS, 2, WIDTH), ((1, 8), (3, 4)), -0.2, 0.2), 0.0, 1.0).astype(jnp.bfloat16),
        "split_beta": jnp.clip(jnp.exp(math.log(0.029907227) - 2.7055024 * jax.random.uniform(arg_keys[3], (SLOTS, 2), jnp.float32) ** levels(arg_keys[3], (SLOTS, 2), ((0, 8),), -0.2, 0.2)), 0.0019989014, 0.029907227).astype(jnp.bfloat16),
        "split_neuron": set_ends(jax.random.randint(arg_keys[4], (SLOTS,), 0, 2 * WIDTH), jax.random.fold_in(arg_keys[4], 1), 0, (2 * WIDTH) - 1).astype(jnp.int32),
        "split_sign": set_ends((jax.random.randint(arg_keys[5], (SLOTS,), 0, 2) < 1).astype(jnp.int32), jax.random.fold_in(arg_keys[5], 1), 0, 1),
        "send_counts": draw_send_counts(jax.random.fold_in(arg_keys[9], 71), 0),
        "spec_row": bell_draw(arg_keys[7], (WIDTH,), (WIDTH * WIDTH) ** -0.5, 0.0007324219, ((0, 4),)),
        "weight": heavy_noise(arg_keys[8], (WIDTH, WIDTH), WIDTH ** -0.5, 0.09375, ((0, 4), (1, 8)), (0, 1, 8, 2.0)),
    }


def relaxation(coeff_in, lower_layer, gap_layer, alpha_layer, beta_rows, neuron_ids, sign_ids, column_ids):
    lower_f = lower_layer.astype(jnp.float32)
    gap_f = gap_layer.astype(jnp.float32)
    upper_f = lower_f + gap_f
    active = lower_f >= 0.0
    inactive = upper_f <= 0.0
    upper_slope = jnp.where(active, 1.0, jnp.where(inactive, 0.0, upper_f / gap_f))
    intercept = jnp.where(active | inactive, 0.0, -upper_f * lower_f / gap_f)
    lower_slope = jnp.where(active[:, None, :], 1.0, jnp.where(inactive[:, None, :], 0.0, alpha_layer.astype(jnp.float32)))
    chosen = neuron_ids[:, None] == column_ids[None, :]
    split_slope = (sign_ids == 1).astype(jnp.float32)
    upper_slope = jnp.where(chosen, split_slope[:, None], upper_slope)
    intercept = jnp.where(chosen, 0.0, intercept)
    lower_slope = jnp.where(chosen[:, None, :], split_slope[:, None, None], lower_slope)
    signed = (2 * sign_ids - 1).astype(jnp.float32)
    penalty = beta_rows.astype(jnp.float32) * signed[:, None]
    positive = jnp.maximum(coeff_in, 0.0)
    negative = jnp.minimum(coeff_in, 0.0)
    result = positive * lower_slope + negative * upper_slope[:, None, :] - chosen[:, None, :].astype(jnp.float32) * penalty[:, :, None]
    offset = jnp.sum(negative * intercept[:, None, :], axis=-1)
    return result, offset


def reference(state_lower, state_gap, state_alpha, split_beta, split_neuron, split_sign, send_counts, spec_row, weight):
    counts = send_counts.astype(jnp.int32)
    out_start = (jnp.cumsum(counts, axis=1) - counts).astype(jnp.int32)
    recv_end = jnp.cumsum(counts, axis=0).astype(jnp.int32)
    recv_start = (recv_end - counts).astype(jnp.int32)
    out_pos = jnp.arange(DOM_DEV, dtype=jnp.int32)
    source = jnp.sum((recv_end.T[:, None, :] <= out_pos[None, :, None]).astype(jnp.int32), axis=2).astype(jnp.int32)
    start_at = jnp.take_along_axis(recv_start.T, source, axis=1)
    send_at = jnp.take_along_axis(out_start.T, source, axis=1)
    row_index = (source * (2 * DOM_DEV) + send_at + out_pos[None, :] - start_at).reshape(-1).astype(jnp.int32)
    moved_lower = jnp.take(state_lower, row_index, axis=1)
    moved_gap = jnp.take(state_gap, row_index, axis=1)
    moved_alpha = jnp.take(state_alpha, row_index, axis=1)
    moved_beta = jnp.take(split_beta, row_index, axis=0)
    moved_tags = jnp.take(jnp.stack([split_neuron, split_sign], axis=1), row_index, axis=0)
    neuron_ids = moved_tags[:, 0]
    sign_ids = moved_tags[:, 1]
    column_ids = jnp.arange(WIDTH, dtype=jnp.int32)
    domain_count = row_index.shape[0]
    spec_sign = jnp.array([1.0, -1.0], dtype=jnp.float32)
    coeff_top = jnp.broadcast_to(spec_sign[None, :, None] * spec_row.astype(jnp.float32)[None, None, :], (domain_count, 2, WIDTH))
    relaxed_top, offset_top = relaxation(coeff_top, moved_lower[1], moved_gap[1], moved_alpha[1], moved_beta, neuron_ids, sign_ids, column_ids + WIDTH)
    coeff_panel = relaxed_top.astype(jnp.bfloat16).reshape(domain_count * 2, WIDTH)
    coeff_low = jnp.dot(coeff_panel, weight, preferred_element_type=jnp.float32).reshape(domain_count, 2, WIDTH)
    relaxed_low, offset_low = relaxation(coeff_low, moved_lower[0], moved_gap[0], moved_alpha[0], moved_beta, neuron_ids, sign_ids, column_ids)
    lower_base = moved_lower[0].astype(jnp.float32)
    upper_base = lower_base + moved_gap[0].astype(jnp.float32)
    box_term = jnp.sum(jnp.maximum(relaxed_low, 0.0) * lower_base[:, None, :] + jnp.minimum(relaxed_low, 0.0) * upper_base[:, None, :], axis=-1)
    totals = offset_top + offset_low + box_term
    bounds = jnp.stack([totals[:, 0], -totals[:, 1]], axis=1)
    return (moved_lower, moved_gap, moved_alpha, moved_beta, neuron_ids, sign_ids, bounds)
```

```python
import jax
import jax.numpy as jnp
from jax import lax
from jax.sharding import PartitionSpec as P

BF = jnp.bfloat16
F32 = jnp.float32


def bit_reverse(value, bits):
    out = 0
    for b in range(bits):
        out |= ((value >> b) & 1) << (bits - 1 - b)
    return out


def pick(matrix, rows):
    return jnp.dot(matrix, rows, preferred_element_type=F32).astype(BF)


def slopes(lower, gap, chosen, split_slope):
    low = lower.astype(F32)
    wide = gap.astype(F32)
    high = low + wide
    active = low >= 0.0
    inactive = high <= 0.0
    ratio = high / wide
    upper_slope = jnp.where(active, 1.0, jnp.where(inactive, 0.0, ratio))
    intercept = jnp.where(active | inactive, 0.0, -high * low / wide)
    upper_slope = jnp.where(chosen, split_slope, upper_slope)
    intercept = jnp.where(chosen, 0.0, intercept)
    return low, high, active, inactive, upper_slope, intercept


def lower_slope_of(alpha, active, inactive, chosen, split_slope):
    slope = jnp.where(active, 1.0, jnp.where(inactive, 0.0, alpha.astype(F32)))
    return jnp.where(chosen, split_slope, slope)


def shards(
    state_lower,
    state_gap,
    state_alpha,
    split_beta,
    split_neuron,
    split_sign,
    send_counts,
    spec_row,
    weight,
):
    groups = lax.axis_size("dom")
    cores = lax.axis_size("neu")
    near = groups // cores
    bits = cores.bit_length() - 1
    assert near * cores == groups and 1 << bits == cores
    device_pos = lax.axis_index("dom")
    core_pos = lax.axis_index("neu")
    slots = state_lower.shape[1]
    rows = slots // 2
    cap = slots // groups
    narrow = state_lower.shape[2]
    width = narrow * cores

    def swap(value, mask):
        return lax.ppermute(value, "dom", [(d, d ^ mask) for d in range(groups)])

    def swap_core(value, mask):
        return lax.ppermute(value, "neu", [(c, c ^ mask) for c in range(cores)])

    counts = send_counts.astype(jnp.int32)
    partner = device_pos ^ jnp.arange(groups, dtype=jnp.int32)
    outgoing = lax.dynamic_index_in_dim(counts, device_pos, 0, keepdims=False)
    incoming = lax.dynamic_index_in_dim(counts, device_pos, 1, keepdims=False)
    out_start = jnp.cumsum(outgoing) - outgoing
    in_start = jnp.cumsum(incoming) - incoming
    match = partner[:, None] == jnp.arange(groups, dtype=jnp.int32)[None, :]
    out_at = jnp.sum(jnp.where(match, out_start[None, :], 0), axis=1)
    in_at = jnp.sum(jnp.where(match, in_start[None, :], 0), axis=1)
    in_count = jnp.sum(jnp.where(match, incoming[None, :], 0), axis=1)
    place = jnp.arange(cap, dtype=jnp.int32)
    slot_of = (out_at[:, None] + place[None, :]).reshape(groups * cap)
    send_mat = (slot_of[:, None] == jnp.arange(slots, dtype=jnp.int32)[None, :]).astype(BF)
    row_of = jnp.where(
        place[None, :] < in_count[:, None], in_at[:, None] + place[None, :], -1
    ).reshape(groups * cap)
    recv_mat = (jnp.arange(rows, dtype=jnp.int32)[:, None] == row_of[None, :]).astype(BF)

    def exchange(plane):
        packed = pick(send_mat, plane).reshape(groups, cap, plane.shape[1])
        parts = [packed[0]] + [swap(packed[k], k) for k in range(1, groups)]
        return pick(recv_mat, jnp.concatenate(parts, axis=0))

    tags = jnp.concatenate(
        [
            (split_neuron >> 7).astype(BF)[:, None],
            (split_neuron & 127).astype(BF)[:, None],
            split_sign.astype(BF)[:, None],
            split_beta,
            jnp.zeros((slots, 123), BF),
        ],
        axis=1,
    )
    positive_spec = (spec_row >= 0)[None, :]
    first, second = state_alpha[1, :, 0, :], state_alpha[1, :, 1, :]
    used = jnp.where(positive_spec, first, second)
    unused = jnp.where(positive_spec, second, first)

    moved_tags = exchange(tags)
    lower_top = exchange(state_lower[1])
    gap_top = exchange(state_gap[1])
    used_top = exchange(used)

    neuron_ids = moved_tags[:, 0].astype(jnp.int32) * 128 + moved_tags[:, 1].astype(jnp.int32)
    sign_ids = moved_tags[:, 2].astype(jnp.int32)
    moved_beta = moved_tags[:, 3:5]
    split_slope = (sign_ids == 1).astype(F32)[:, None]
    penalty = moved_beta.astype(F32) * (2 * sign_ids - 1).astype(F32)[:, None]
    columns = core_pos * narrow + jnp.arange(narrow, dtype=jnp.int32)

    panel = weight
    step = 1
    while step < near:
        other = swap(panel, step)
        low_side = (device_pos & step) == 0
        panel = jnp.concatenate(
            [jnp.where(low_side, panel, other), jnp.where(low_side, other, panel)], axis=1
        )
        step *= 2

    chosen = neuron_ids[:, None] == (columns + width)[None, :]
    low, high, active, inactive, upper_slope, intercept = slopes(
        lower_top, gap_top, chosen, split_slope
    )
    lower_slope = lower_slope_of(used_top, active, inactive, chosen, split_slope)
    spec = spec_row.astype(F32)[None, :]
    hit = chosen.astype(F32)
    relaxed_top = []
    offset = []
    for s in range(2):
        coeff = spec if s == 0 else -spec
        value = jnp.maximum(coeff, 0.0) * lower_slope + jnp.minimum(coeff, 0.0) * upper_slope
        relaxed_top.append((value - hit * penalty[:, s : s + 1]).astype(BF))
        offset.append(jnp.sum(jnp.minimum(coeff, 0.0) * intercept, axis=1))
    mine = jnp.concatenate(relaxed_top, axis=0)

    held = {0: mine}
    for b in reversed(range(bits)):
        for delta in list(held):
            held[delta | (1 << b)] = swap(held[delta], near << b)
    partial = jnp.stack(
        [jnp.dot(held[d], panel, preferred_element_type=F32) for d in range(cores)]
    )

    for b in range(bits):
        side = (core_pos >> b) & 1
        half = partial.shape[0] // 2
        keep = lax.dynamic_slice_in_dim(partial, side * half, half, 0)
        give = lax.dynamic_slice_in_dim(partial, (1 - side) * half, half, 0)
        partial = keep + swap_core(give.astype(BF), 1 << b).astype(F32)
    route = []
    for o in range(cores):
        for x in range(near):
            for c in range(cores):
                to = o ^ bit_reverse(c, bits)
                route.append(((o * near + x) * cores + c, (to * near + x) * cores + o))
    coeff_low = lax.ppermute(partial[0].astype(BF), ("dom", "neu"), route).astype(F32)

    lower_low = exchange(state_lower[0])
    gap_low = exchange(state_gap[0])
    alpha_low = [exchange(state_alpha[0, :, s, :]) for s in range(2)]
    unused_top = exchange(unused)

    chosen = neuron_ids[:, None] == columns[None, :]
    low, high, active, inactive, upper_slope, intercept = slopes(
        lower_low, gap_low, chosen, split_slope
    )
    hit = chosen.astype(F32)
    for s in range(2):
        coeff = coeff_low[s * rows : (s + 1) * rows]
        lower_slope = lower_slope_of(alpha_low[s], active, inactive, chosen, split_slope)
        negative = jnp.minimum(coeff, 0.0)
        value = jnp.maximum(coeff, 0.0) * lower_slope + negative * upper_slope
        value = value - hit * penalty[:, s : s + 1]
        offset[s] = offset[s] + jnp.sum(
            negative * intercept + jnp.maximum(value, 0.0) * low + jnp.minimum(value, 0.0) * high,
            axis=1,
        )
    totals = lax.psum(jnp.stack(offset, axis=1), "neu")
    bounds = jnp.stack([totals[:, 0], -totals[:, 1]], axis=1)

    alpha_top = [
        jnp.where(positive_spec, used_top, unused_top),
        jnp.where(positive_spec, unused_top, used_top),
    ]
    moved_lower = jnp.stack([lower_low, lower_top])
    moved_gap = jnp.stack([gap_low, gap_top])
    moved_alpha = jnp.stack([jnp.stack(alpha_low, axis=1), jnp.stack(alpha_top, axis=1)])
    return (moved_lower, moved_gap, moved_alpha, moved_beta, neuron_ids, sign_ids, bounds)


def solution(mesh):
    in_specs = (
        P(None, "dom", "neu"),
        P(None, "dom", "neu"),
        P(None, "dom", None, "neu"),
        P("dom", None),
        P("dom"),
        P("dom"),
        P(),
        P("neu"),
        P("neu", "dom"),
    )
    out_specs = (
        P(None, "dom", "neu"),
        P(None, "dom", "neu"),
        P(None, "dom", None, "neu"),
        P("dom", None),
        P("dom"),
        P("dom"),
        P("dom", None),
    )
    return jax.shard_map(shards, mesh=mesh, in_specs=in_specs, out_specs=out_specs, check_vma=False)
```

```python
import functools

import jax
import jax.numpy as jnp
from jax import lax
from jax.experimental import pallas as pl
from jax.experimental.pallas import tpu as pltpu
from jax.sharding import PartitionSpec as P

BF = jnp.bfloat16
F32 = jnp.float32
I32 = jnp.int32
TAGS = 8
LANES = 128
VMEM_BYTES = 48 << 20


def bit_reverse(value, bits):
    out = 0
    for b in range(bits):
        out |= ((value >> b) & 1) << (bits - 1 - b)
    return out


def tile_of(narrow):
    return min(512, narrow)


def dot(a, b):
    return jnp.dot(a, b, preferred_element_type=F32)


def dot_nt(a, b):
    return lax.dot_general(a, b, (((1,), (1,)), ((), ())), preferred_element_type=F32)


def spread(values, index, cap):
    out = jnp.zeros(index.shape, I32)
    for k, value in enumerate(values):
        inside = (index >= k * cap) & (index < (k + 1) * cap)
        out = jnp.where(inside, value, out)
    return out


def prefix(counts_ref, row, end, groups):
    total = jnp.int32(0)
    for e in range(groups - 1):
        total = total + jnp.where(e < end, counts_ref[row, e], 0)
    return total


def column_prefix(counts_ref, column, end, groups):
    total = jnp.int32(0)
    for d in range(groups - 1):
        total = total + jnp.where(d < end, counts_ref[d, column], 0)
    return total


def partners(swapped, groups):
    me = lax.axis_index("dom")
    return [me ^ k if swapped else k for k in range(groups)]


def send_matrix(counts_ref, swapped, groups, cap, slots):
    me = lax.axis_index("dom")
    other = partners(swapped, groups)
    places = groups * cap
    place = lax.broadcasted_iota(I32, (places, 1), 0)
    shift = [prefix(counts_ref, me, other[k], groups) - k * cap for k in range(groups)]
    slot = lax.broadcasted_iota(I32, (places, slots), 1)
    return (slot == place + spread(shift, place, cap)).astype(BF)


def settle_matrix(counts_ref, swapped, groups, cap, rows):
    me = lax.axis_index("dom")
    places = groups * cap
    place = lax.broadcasted_iota(I32, (1, places), 1)
    shift, limit = [], []
    for k, partner in enumerate(partners(swapped, groups)):
        shift.append(column_prefix(counts_ref, me, partner, groups) - k * cap)
        limit.append(counts_ref[partner, me] + k * cap)
    target = jnp.where(place < spread(limit, place, cap), place + spread(shift, place, cap), -1)
    row = lax.broadcasted_iota(I32, (rows, places), 0)
    return (row == target).astype(BF)


def pool_pack_kernel(groups, cap, counts_ref, *refs):
    sources, out_refs, mat_ref = refs[: -groups - 1], refs[-groups - 1 : -1], refs[-1]
    slots = mat_ref.shape[1]

    @pl.when(pl.program_id(0) == 0)
    def _():
        mat_ref[...] = send_matrix(counts_ref, True, groups, cap, slots)

    mat = mat_ref[...]
    for p, plane in enumerate(pool_planes(*sources)):
        packed = dot(mat, plane).reshape(groups, cap, plane.shape[1]).astype(BF)
        for k in range(groups):
            out_refs[k][p] = packed[k]


def top_pack_kernel(groups, cap, counts_ref, tags_ref, *refs):
    sources, out_ref, mat_ref = refs[:-2], refs[-2], refs[-1]
    slots = mat_ref.shape[1]

    @pl.when(pl.program_id(0) == 0)
    def _():
        mat_ref[...] = send_matrix(counts_ref, False, groups, cap, slots)
        me = lax.axis_index("dom")
        place = lax.broadcasted_iota(I32, (LANES, slots), 0)
        slot = lax.broadcasted_iota(I32, (LANES, slots), 1)
        for e in range(groups):
            hit = (slot == place + prefix(counts_ref, me, e, groups)).astype(BF)
            out_ref[e, 3 * cap :, 0:LANES] = dot_nt(tags_ref[...], hit).astype(BF)

    mat = mat_ref[...]
    for p, plane in enumerate(top_planes(*sources)):
        packed = dot(mat, plane).reshape(groups, cap, plane.shape[1])
        out_ref[:, p * cap : (p + 1) * cap] = packed.astype(BF)


def either(spec_ref, first, second):
    side = spec_ref[...].astype(F32) >= 0.0
    return jnp.where(side, first.astype(F32), second.astype(F32)).astype(BF)


def used_alpha(alpha_ref, spec_ref):
    return either(spec_ref, alpha_ref[0, :, 0, :], alpha_ref[0, :, 1, :])


def unused_alpha(alpha_ref, spec_ref):
    return either(spec_ref, alpha_ref[0, :, 1, :], alpha_ref[0, :, 0, :])


def top_planes(lower_ref, gap_ref, alpha_ref, spec_ref):
    return [lower_ref[0], gap_ref[0], used_alpha(alpha_ref, spec_ref)]


def pool_planes(lower_ref, gap_ref, alpha_ref, top_alpha_ref, spec_ref):
    return [
        lower_ref[0],
        gap_ref[0],
        alpha_ref[0, :, 0, :],
        alpha_ref[0, :, 1, :],
        unused_alpha(top_alpha_ref, spec_ref),
    ]


def slopes(low, gap, chosen, split_slope):
    high = low + gap
    active = low >= 0.0
    inactive = high <= 0.0
    ratio = high / gap
    upper_slope = jnp.where(active, 1.0, jnp.where(inactive, 0.0, ratio))
    intercept = jnp.where(active | inactive | chosen, 0.0, -ratio * low)
    upper_slope = jnp.where(chosen, split_slope, upper_slope)
    return high, active, inactive, upper_slope, intercept


def lower_slope_of(alpha, active, inactive, chosen, split_slope):
    slope = jnp.where(active, 1.0, jnp.where(inactive, 0.0, alpha))
    return jnp.where(chosen, split_slope, slope)


def row_facts(tags):
    neuron = tags[:, 0:1] * 128.0 + tags[:, 1:2]
    active_branch = tags[:, 2:3]
    split_slope = jnp.where(active_branch == 1.0, 1.0, 0.0)
    penalty = [tags[:, 3 + s : 4 + s] * (2.0 * active_branch - 1.0) for s in range(2)]
    return neuron.astype(I32), split_slope, penalty


def stacked(in_refs, plane):
    return jnp.concatenate([ref[plane] for ref in in_refs], axis=0)


def top_kernel(groups, cap, counts_ref, in_ref, spec_ref, *refs):
    lower_ref, gap_ref, used_ref, relaxed_ref, moved_ref, offset_ref, mat_ref = refs
    rows, tile = used_ref.shape
    step = pl.program_id(0)
    narrow = tile * pl.num_programs(0)

    @pl.when(step == 0)
    def _():
        mat_ref[...] = settle_matrix(counts_ref, False, groups, cap, rows)
        me = lax.axis_index("dom")
        row = lax.broadcasted_iota(I32, (rows, LANES), 0)
        place = lax.broadcasted_iota(I32, (rows, LANES), 1)
        moved = jnp.zeros((rows, TAGS), F32)
        for d in range(groups):
            first = column_prefix(counts_ref, me, d, groups)
            hit = ((row - place == first) & (place < counts_ref[d, me])).astype(BF)
            moved = moved + dot_nt(hit, in_ref[d, 3 * cap :, 0:LANES])
        moved_ref[...] = moved
        offset_ref[...] = jnp.zeros_like(offset_ref)

    mat = mat_ref[...]
    low, gap, used = (
        dot(mat, in_ref[:, p * cap : (p + 1) * cap].reshape(groups * cap, tile)) for p in range(3)
    )
    lower_ref[0] = low.astype(BF)
    gap_ref[0] = gap.astype(BF)
    used_ref[...] = used.astype(BF)
    neuron, split_slope, penalty = row_facts(moved_ref[...])
    base = (lax.axis_index("neu") + lax.axis_size("neu")) * narrow + step * tile
    chosen = neuron == base + lax.broadcasted_iota(I32, (rows, tile), 1)
    high, active, inactive, upper_slope, intercept = slopes(low, gap, chosen, split_slope)
    lower_slope = lower_slope_of(used, active, inactive, chosen, split_slope)
    spec = spec_ref[...].astype(F32)
    sums = []
    for s in range(2):
        coeff = spec if s == 0 else -spec
        negative = jnp.minimum(coeff, 0.0)
        value = jnp.maximum(coeff, 0.0) * lower_slope + negative * upper_slope
        value = value - jnp.where(chosen, penalty[s], 0.0)
        relaxed_ref[s] = value.astype(BF)
        sums.append(jnp.sum(negative * intercept, axis=1, keepdims=True))
    offset_ref[...] += jnp.concatenate(sums, axis=1)


def low_kernel(groups, cap, counts_ref, *refs):
    in_refs, refs = refs[:groups], refs[groups:]
    coeff_ref, tags_ref, before_ref, used_ref, spec_ref, _, _, *refs = refs
    lower_ref, gap_ref, alpha_ref, offset_ref, mat_ref = refs
    rows, tile = used_ref.shape
    step = pl.program_id(0)
    narrow = tile * pl.num_programs(0)

    @pl.when(step == 0)
    def _():
        mat_ref[...] = settle_matrix(counts_ref, True, groups, cap, rows)
        offset_ref[...] = before_ref[...]

    mat = mat_ref[...]
    low, gap, *alpha, rest = (dot(mat, stacked(in_refs, p)) for p in range(5))
    lower_ref[0] = low.astype(BF)
    gap_ref[0] = gap.astype(BF)
    for s in range(2):
        alpha_ref[0, :, s, :] = alpha[s].astype(BF)
    used = used_ref[...]
    alpha_ref[1, :, 0, :] = either(spec_ref, used, rest)
    alpha_ref[1, :, 1, :] = either(spec_ref, rest, used)
    neuron, split_slope, penalty = row_facts(tags_ref[...])
    base = lax.axis_index("neu") * narrow + step * tile
    chosen = neuron == base + lax.broadcasted_iota(I32, (rows, tile), 1)
    high, active, inactive, upper_slope, intercept = slopes(low, gap, chosen, split_slope)
    sums = []
    for s in range(2):
        coeff = coeff_ref[s].astype(F32)
        lower_slope = lower_slope_of(alpha[s], active, inactive, chosen, split_slope)
        negative = jnp.minimum(coeff, 0.0)
        value = jnp.maximum(coeff, 0.0) * lower_slope + negative * upper_slope
        value = value - jnp.where(chosen, penalty[s], 0.0)
        term = negative * intercept + jnp.maximum(value, 0.0) * low + jnp.minimum(value, 0.0) * high
        sums.append(jnp.sum(term, axis=1, keepdims=True))
    offset_ref[...] += jnp.concatenate(sums, axis=1)


def shards(
    state_lower,
    state_gap,
    state_alpha,
    split_beta,
    split_neuron,
    split_sign,
    send_counts,
    spec_row,
    weight,
):
    groups = lax.axis_size("dom")
    cores = lax.axis_size("neu")
    near = groups // cores
    bits = cores.bit_length() - 1
    assert near * cores == groups and 1 << bits == cores
    device_pos = lax.axis_index("dom")
    core_pos = lax.axis_index("neu")
    slots = state_lower.shape[1]
    rows = slots // 2
    cap = slots // groups
    places = groups * cap
    narrow = state_lower.shape[2]
    tile = tile_of(narrow)
    grid = (narrow // tile,)
    counts = send_counts.astype(I32)
    spec = spec_row[None, :]
    params = pltpu.CompilerParams(vmem_limit_bytes=VMEM_BYTES)

    smem = pl.BlockSpec(memory_space=pltpu.SMEM)

    def plane_spec(layer, count):
        return pl.BlockSpec((1, count, tile), lambda i: (layer, 0, i))

    def pair_spec(layer, count):
        return pl.BlockSpec((1, count, 2, tile), lambda i: (layer, 0, 0, i))

    def part_spec(planes):
        return pl.BlockSpec((planes, cap, tile), lambda i: (0, 0, i))

    def whole(*shape):
        return pl.BlockSpec(shape, lambda i: (0,) * len(shape))

    spec_spec = pl.BlockSpec((1, tile), lambda i: (0, i))
    flat_spec = pl.BlockSpec((rows, tile), lambda i: (0, i))
    both_spec = pl.BlockSpec((2, rows, tile), lambda i: (0, 0, i))

    def swap(value, mask):
        return lax.ppermute(value, "dom", [(d, d ^ mask) for d in range(groups)])

    def swap_core(value, mask):
        return lax.ppermute(value, "neu", [(c, c ^ mask) for c in range(cores)])

    def after(value, *others):
        return lax.optimization_barrier((value,) + others)[0]

    tags = jnp.concatenate(
        [
            (split_neuron >> 7).astype(BF)[None],
            (split_neuron & 127).astype(BF)[None],
            split_sign.astype(BF)[None],
            split_beta.T,
            jnp.zeros((TAGS - 5, slots), BF),
        ],
        axis=0,
    )
    top_rows = 3 * cap + TAGS
    top_spec = pl.BlockSpec((groups, top_rows, tile), lambda i: (0, 0, i))
    packed_top = pl.pallas_call(
        functools.partial(top_pack_kernel, groups, cap),
        grid=grid,
        in_specs=[
            smem,
            whole(TAGS, slots),
            plane_spec(1, slots),
            plane_spec(1, slots),
            pair_spec(1, slots),
            spec_spec,
        ],
        out_specs=top_spec,
        out_shape=jax.ShapeDtypeStruct((groups, top_rows, narrow), BF),
        scratch_shapes=[pltpu.VMEM((places, slots), BF)],
        compiler_params=params,
    )(counts, tags, state_lower, state_gap, state_alpha, spec)
    in_top = lax.all_to_all(packed_top, "dom", split_axis=0, concat_axis=0, tiled=True)

    pool = pl.pallas_call(
        functools.partial(pool_pack_kernel, groups, cap),
        grid=grid,
        in_specs=[
            smem,
            plane_spec(0, slots),
            plane_spec(0, slots),
            pair_spec(0, slots),
            pair_spec(1, slots),
            spec_spec,
        ],
        out_specs=[part_spec(5)] * groups,
        out_shape=[jax.ShapeDtypeStruct((5, cap, narrow), BF)] * groups,
        scratch_shapes=[pltpu.VMEM((places, slots), BF)],
        compiler_params=params,
    )(counts, state_lower, state_gap, state_alpha, state_alpha, spec)

    panel = after(weight, in_top, pool[0])
    near_panels = []
    step = 1
    while step < near:
        other = swap(panel, step)
        near_panels.append(other)
        low_side = (device_pos & step) == 0
        panel = jnp.concatenate(
            [jnp.where(low_side, panel, other), jnp.where(low_side, other, panel)], axis=1
        )
        step *= 2

    in_top, pool = lax.optimization_barrier((in_top, pool))
    moved_lower, moved_gap, used_top, relaxed_top, moved_tags, offset = pl.pallas_call(
        functools.partial(top_kernel, groups, cap),
        grid=grid,
        in_specs=[smem, top_spec, spec_spec],
        out_specs=[
            plane_spec(1, rows),
            plane_spec(1, rows),
            flat_spec,
            both_spec,
            whole(rows, TAGS),
            whole(rows, 2),
        ],
        out_shape=[
            jax.ShapeDtypeStruct((2, rows, narrow), BF),
            jax.ShapeDtypeStruct((2, rows, narrow), BF),
            jax.ShapeDtypeStruct((rows, narrow), BF),
            jax.ShapeDtypeStruct((2, rows, narrow), BF),
            jax.ShapeDtypeStruct((rows, TAGS), F32),
            jax.ShapeDtypeStruct((rows, 2), F32),
        ],
        scratch_shapes=[pltpu.VMEM((rows, places), BF)],
        compiler_params=params,
    )(counts, in_top, spec)

    half = groups // 2
    order = list(range(half, groups)) + list(range(near, half)) + list(range(1, near))
    cut = [0, groups // 8, 3 * groups // 8, 5 * groups // 8, groups - 1]
    arrived = {0: pool[0]}

    def send_pool(stage, ready, *others):
        parts = order[cut[stage] : cut[stage + 1]]
        for k in parts:
            arrived[k] = swap(after(pool[k], *others), k)
        return after(ready, *[arrived[k] for k in parts])

    held = {0: relaxed_top.reshape(2 * rows, narrow)}
    for b in reversed(range(bits)):
        for delta in [d for d in held if d | (1 << b) not in held]:
            held[delta | (1 << b)] = swap(held[delta], near << b)
        if b == bits - 1:
            held[1 << b] = send_pool(0, held[1 << b], in_top)
            if bits > 1:
                held[1] = swap(held[0], near)
                held[1 << b] = after(held[1 << b], held[1], *near_panels)
    held[cores - 1] = send_pool(1, held[cores - 1], held[cores // 2])
    partial = jnp.stack([dot(held[d], panel).astype(BF) for d in range(cores)])

    for b in range(bits):
        side = (core_pos >> b) & 1
        half = partial.shape[0] // 2
        keep = lax.dynamic_slice_in_dim(partial, side * half, half, 0)
        give = lax.dynamic_slice_in_dim(partial, (1 - side) * half, half, 0)
        taken = swap_core(give, 1 << b)
        if b == bits - 1:
            taken = send_pool(2, taken, give)
        partial = (keep.astype(F32) + taken.astype(F32)).astype(BF)
    route = []
    for o in range(cores):
        for x in range(near):
            for c in range(cores):
                to = o ^ bit_reverse(c, bits)
                route.append(((o * near + x) * cores + c, (to * near + x) * cores + o))
    coeff_low = lax.ppermute(partial[0], ("dom", "neu"), route)

    coeff_low = send_pool(3, coeff_low, partial)

    hbm = pl.BlockSpec(memory_space=pl.ANY)
    moved_lower, moved_gap, moved_alpha, offset = pl.pallas_call(
        functools.partial(low_kernel, groups, cap),
        grid=grid,
        in_specs=[smem]
        + [part_spec(5)] * groups
        + [both_spec, whole(rows, TAGS), whole(rows, 2), flat_spec, spec_spec, hbm, hbm],
        out_specs=[
            plane_spec(0, rows),
            plane_spec(0, rows),
            pl.BlockSpec((2, rows, 2, tile), lambda i: (0, 0, 0, i)),
            whole(rows, 2),
        ],
        out_shape=[
            jax.ShapeDtypeStruct((2, rows, narrow), BF),
            jax.ShapeDtypeStruct((2, rows, narrow), BF),
            jax.ShapeDtypeStruct((2, rows, 2, narrow), BF),
            jax.ShapeDtypeStruct((rows, 2), F32),
        ],
        input_output_aliases={groups + 6: 0, groups + 7: 1},
        scratch_shapes=[pltpu.VMEM((rows, places), BF)],
        compiler_params=params,
    )(
        counts,
        *[arrived[k] for k in range(groups)],
        coeff_low.reshape(2, rows, narrow),
        moved_tags,
        offset,
        used_top,
        spec,
        moved_lower,
        moved_gap,
    )

    totals = lax.psum(offset, "neu")
    bounds = jnp.stack([totals[:, 0], -totals[:, 1]], axis=1)
    neuron_ids = moved_tags[:, 0].astype(I32) * 128 + moved_tags[:, 1].astype(I32)
    sign_ids = moved_tags[:, 2].astype(I32)
    moved_beta = moved_tags[:, 3:5].astype(BF)
    return (moved_lower, moved_gap, moved_alpha, moved_beta, neuron_ids, sign_ids, bounds)


def solution(mesh):
    in_specs = (
        P(None, "dom", "neu"),
        P(None, "dom", "neu"),
        P(None, "dom", None, "neu"),
        P("dom", None),
        P("dom"),
        P("dom"),
        P(),
        P("neu"),
        P("neu", "dom"),
    )
    out_specs = (
        P(None, "dom", "neu"),
        P(None, "dom", "neu"),
        P(None, "dom", None, "neu"),
        P("dom", None),
        P("dom"),
        P("dom"),
        P("dom", None),
    )
    return jax.shard_map(shards, mesh=mesh, in_specs=in_specs, out_specs=out_specs, check_vma=False)
```

```python
import functools

import jax
import jax.numpy as jnp
from jax import lax
from jax.experimental import pallas as pl
from jax.experimental.pallas import tpu as pltpu
from jax.sharding import PartitionSpec as P

BF = jnp.bfloat16
F32 = jnp.float32
I32 = jnp.int32
TAGS = 8
LANES = 128
LOW_PLANES = 4
PLANES = 5
VMEM_BYTES = 48 << 20


def bit_reverse(value, bits):
    out = 0
    for b in range(bits):
        out |= ((value >> b) & 1) << (bits - 1 - b)
    return out


def tile_of(narrow):
    return min(512, narrow)


def dot(a, b):
    return jnp.dot(a, b, preferred_element_type=F32)


def dot_nt(a, b):
    return lax.dot_general(a, b, (((1,), (1,)), ((), ())), preferred_element_type=F32)


def spread(values, index, cap):
    out = jnp.zeros(index.shape, I32)
    for k, value in enumerate(values):
        inside = (index >= k * cap) & (index < (k + 1) * cap)
        out = jnp.where(inside, value, out)
    return out


def prefix(counts_ref, row, end, groups):
    total = jnp.int32(0)
    for e in range(groups - 1):
        total = total + jnp.where(e < end, counts_ref[row, e], 0)
    return total


def column_prefix(counts_ref, column, end, groups):
    total = jnp.int32(0)
    for d in range(groups - 1):
        total = total + jnp.where(d < end, counts_ref[d, column], 0)
    return total


def partners(swapped, groups):
    me = lax.axis_index("dom")
    return [me ^ k if swapped else k for k in range(groups)]


def send_matrix(counts_ref, swapped, groups, cap, slots):
    me = lax.axis_index("dom")
    other = partners(swapped, groups)
    places = groups * cap
    place = lax.broadcasted_iota(I32, (places, 1), 0)
    shift = [prefix(counts_ref, me, other[k], groups) - k * cap for k in range(groups)]
    slot = lax.broadcasted_iota(I32, (places, slots), 1)
    return (slot == place + spread(shift, place, cap)).astype(BF)


def settle_matrix(counts_ref, swapped, groups, cap, rows):
    me = lax.axis_index("dom")
    places = groups * cap
    place = lax.broadcasted_iota(I32, (1, places), 1)
    shift, limit = [], []
    for k, partner in enumerate(partners(swapped, groups)):
        shift.append(column_prefix(counts_ref, me, partner, groups) - k * cap)
        limit.append(counts_ref[partner, me] + k * cap)
    target = jnp.where(place < spread(limit, place, cap), place + spread(shift, place, cap), -1)
    row = lax.broadcasted_iota(I32, (rows, places), 0)
    return (row == target).astype(BF)


def pool_pack_kernel(groups, cap, counts_ref, *refs):
    sources, out_refs, mat_ref = refs[: -groups - 1], refs[-groups - 1 : -1], refs[-1]
    slots = mat_ref.shape[1]

    @pl.when(pl.program_id(0) == 0)
    def _():
        mat_ref[...] = send_matrix(counts_ref, True, groups, cap, slots)

    mat = mat_ref[...]
    for p, plane in enumerate(pool_planes(*sources)):
        packed = dot(mat, plane).reshape(groups, cap, plane.shape[1]).astype(BF)
        for k in range(groups):
            out_refs[k][p] = packed[k]


def top_pack_kernel(groups, cap, counts_ref, tags_ref, *refs):
    sources, out_ref, mat_ref = refs[:-2], refs[-2], refs[-1]
    slots = mat_ref.shape[1]

    @pl.when(pl.program_id(0) == 0)
    def _():
        mat_ref[...] = send_matrix(counts_ref, False, groups, cap, slots)
        me = lax.axis_index("dom")
        place = lax.broadcasted_iota(I32, (LANES, slots), 0)
        slot = lax.broadcasted_iota(I32, (LANES, slots), 1)
        for e in range(groups):
            hit = (slot == place + prefix(counts_ref, me, e, groups)).astype(BF)
            out_ref[e, 3 * cap :, 0:LANES] = dot_nt(tags_ref[...], hit).astype(BF)

    mat = mat_ref[...]
    for p, plane in enumerate(top_planes(*sources)):
        packed = dot(mat, plane).reshape(groups, cap, plane.shape[1])
        out_ref[:, p * cap : (p + 1) * cap] = packed.astype(BF)


def either(spec_ref, first, second):
    side = spec_ref[...].astype(F32) >= 0.0
    return jnp.where(side, first.astype(F32), second.astype(F32)).astype(BF)


def used_alpha(alpha_ref, spec_ref):
    return either(spec_ref, alpha_ref[0, :, 0, :], alpha_ref[0, :, 1, :])


def unused_alpha(alpha_ref, spec_ref):
    return either(spec_ref, alpha_ref[0, :, 1, :], alpha_ref[0, :, 0, :])


def top_planes(lower_ref, gap_ref, alpha_ref, spec_ref):
    return [lower_ref[0], gap_ref[0], used_alpha(alpha_ref, spec_ref)]


def pool_planes(lower_ref, gap_ref, alpha_ref, top_alpha_ref, spec_ref):
    return [
        lower_ref[0],
        gap_ref[0],
        alpha_ref[0, :, 0, :],
        alpha_ref[0, :, 1, :],
        unused_alpha(top_alpha_ref, spec_ref),
    ]


def slopes(low, gap, chosen, split_slope):
    high = low + gap
    active = low >= 0.0
    inactive = high <= 0.0
    ratio = high / gap
    upper_slope = jnp.where(active, 1.0, jnp.where(inactive, 0.0, ratio))
    intercept = jnp.where(active | inactive | chosen, 0.0, -ratio * low)
    upper_slope = jnp.where(chosen, split_slope, upper_slope)
    return high, active, inactive, upper_slope, intercept


def lower_slope_of(alpha, active, inactive, chosen, split_slope):
    slope = jnp.where(active, 1.0, jnp.where(inactive, 0.0, alpha))
    return jnp.where(chosen, split_slope, slope)


def row_facts(tags):
    neuron = tags[:, 0:1] * 128.0 + tags[:, 1:2]
    active_branch = tags[:, 2:3]
    split_slope = jnp.where(active_branch == 1.0, 1.0, 0.0)
    penalty = [tags[:, 3 + s : 4 + s] * (2.0 * active_branch - 1.0) for s in range(2)]
    return neuron.astype(I32), split_slope, penalty


def stacked(in_refs, plane):
    return jnp.concatenate([ref[plane] for ref in in_refs], axis=0)


def top_kernel(groups, cap, counts_ref, in_ref, spec_ref, *refs):
    lower_ref, gap_ref, used_ref, relaxed_ref, moved_ref, offset_ref, mat_ref = refs
    rows, tile = used_ref.shape
    step = pl.program_id(0)
    narrow = tile * pl.num_programs(0)

    @pl.when(step == 0)
    def _():
        mat_ref[...] = settle_matrix(counts_ref, False, groups, cap, rows)
        me = lax.axis_index("dom")
        row = lax.broadcasted_iota(I32, (rows, LANES), 0)
        place = lax.broadcasted_iota(I32, (rows, LANES), 1)
        moved = jnp.zeros((rows, TAGS), F32)
        for d in range(groups):
            first = column_prefix(counts_ref, me, d, groups)
            hit = ((row - place == first) & (place < counts_ref[d, me])).astype(BF)
            moved = moved + dot_nt(hit, in_ref[d, 3 * cap :, 0:LANES])
        moved_ref[...] = moved
        offset_ref[...] = jnp.zeros_like(offset_ref)

    mat = mat_ref[...]
    low, gap, used = (
        dot(mat, in_ref[:, p * cap : (p + 1) * cap].reshape(groups * cap, tile)) for p in range(3)
    )
    lower_ref[0] = low.astype(BF)
    gap_ref[0] = gap.astype(BF)
    used_ref[...] = used.astype(BF)
    neuron, split_slope, penalty = row_facts(moved_ref[...])
    base = (lax.axis_index("neu") + lax.axis_size("neu")) * narrow + step * tile
    chosen = neuron == base + lax.broadcasted_iota(I32, (rows, tile), 1)
    high, active, inactive, upper_slope, intercept = slopes(low, gap, chosen, split_slope)
    lower_slope = lower_slope_of(used, active, inactive, chosen, split_slope)
    spec = spec_ref[...].astype(F32)
    sums = []
    for s in range(2):
        coeff = spec if s == 0 else -spec
        negative = jnp.minimum(coeff, 0.0)
        value = jnp.maximum(coeff, 0.0) * lower_slope + negative * upper_slope
        value = value - jnp.where(chosen, penalty[s], 0.0)
        relaxed_ref[s] = value.astype(BF)
        sums.append(jnp.sum(negative * intercept, axis=1, keepdims=True))
    offset_ref[...] += jnp.concatenate(sums, axis=1)


def settle_kernel(groups, cap, counts_ref, *refs):
    in_refs, refs = refs[:groups], refs[groups:]
    _, _, lower_ref, gap_ref, alpha_ref, mat_ref = refs
    rows = mat_ref.shape[0]

    @pl.when(pl.program_id(0) == 0)
    def _():
        mat_ref[...] = settle_matrix(counts_ref, True, groups, cap, rows)

    mat = mat_ref[...]
    low, gap, *alpha = (
        dot(mat, stacked(in_refs, p)).astype(BF) for p in range(LOW_PLANES)
    )
    lower_ref[0] = low
    gap_ref[0] = gap
    for s in range(2):
        alpha_ref[0, :, s, :] = alpha[s]


def rest_kernel(groups, cap, counts_ref, *refs):
    in_refs, (used_ref, spec_ref, _, alpha_ref, mat_ref) = refs[:groups], refs[groups:]
    rows = mat_ref.shape[0]

    @pl.when(pl.program_id(0) == 0)
    def _():
        mat_ref[...] = settle_matrix(counts_ref, True, groups, cap, rows)

    rest = dot(mat_ref[...], stacked(in_refs, 0)).astype(BF)
    used = used_ref[...]
    alpha_ref[0, :, 0, :] = either(spec_ref, used, rest)
    alpha_ref[0, :, 1, :] = either(spec_ref, rest, used)


def low_kernel(coeff_ref, tags_ref, before_ref, lower_ref, gap_ref, alpha_ref, offset_ref):
    rows, tile = lower_ref.shape[1:]
    step = pl.program_id(0)
    narrow = tile * pl.num_programs(0)

    @pl.when(step == 0)
    def _():
        offset_ref[...] = before_ref[...]

    low = lower_ref[0].astype(F32)
    gap = gap_ref[0].astype(F32)
    neuron, split_slope, penalty = row_facts(tags_ref[...])
    base = lax.axis_index("neu") * narrow + step * tile
    chosen = neuron == base + lax.broadcasted_iota(I32, (rows, tile), 1)
    high, active, inactive, upper_slope, intercept = slopes(low, gap, chosen, split_slope)
    sums = []
    for s in range(2):
        alpha = alpha_ref[0, :, s, :].astype(F32)
        coeff = coeff_ref[s].astype(F32)
        lower_slope = lower_slope_of(alpha, active, inactive, chosen, split_slope)
        negative = jnp.minimum(coeff, 0.0)
        value = jnp.maximum(coeff, 0.0) * lower_slope + negative * upper_slope
        value = value - jnp.where(chosen, penalty[s], 0.0)
        term = negative * intercept + jnp.maximum(value, 0.0) * low + jnp.minimum(value, 0.0) * high
        sums.append(jnp.sum(term, axis=1, keepdims=True))
    offset_ref[...] += jnp.concatenate(sums, axis=1)


def shards(
    state_lower,
    state_gap,
    state_alpha,
    split_beta,
    split_neuron,
    split_sign,
    send_counts,
    spec_row,
    weight,
):
    groups = lax.axis_size("dom")
    cores = lax.axis_size("neu")
    near = groups // cores
    bits = cores.bit_length() - 1
    assert near * cores == groups and 1 << bits == cores
    device_pos = lax.axis_index("dom")
    core_pos = lax.axis_index("neu")
    slots = state_lower.shape[1]
    rows = slots // 2
    cap = slots // groups
    places = groups * cap
    narrow = state_lower.shape[2]
    tile = tile_of(narrow)
    grid = (narrow // tile,)
    counts = send_counts.astype(I32)
    spec = spec_row[None, :]
    params = pltpu.CompilerParams(vmem_limit_bytes=VMEM_BYTES)

    smem = pl.BlockSpec(memory_space=pltpu.SMEM)

    def plane_spec(layer, count):
        return pl.BlockSpec((1, count, tile), lambda i: (layer, 0, i))

    def pair_spec(layer, count):
        return pl.BlockSpec((1, count, 2, tile), lambda i: (layer, 0, 0, i))

    def part_spec(planes):
        return pl.BlockSpec((planes, cap, tile), lambda i: (0, 0, i))

    def whole(*shape):
        return pl.BlockSpec(shape, lambda i: (0,) * len(shape))

    spec_spec = pl.BlockSpec((1, tile), lambda i: (0, i))
    flat_spec = pl.BlockSpec((rows, tile), lambda i: (0, i))
    both_spec = pl.BlockSpec((2, rows, tile), lambda i: (0, 0, i))

    def swap(value, mask):
        return lax.ppermute(value, "dom", [(d, d ^ mask) for d in range(groups)])

    def swap_core(value, mask):
        return lax.ppermute(value, "neu", [(c, c ^ mask) for c in range(cores)])

    def after(value, *others):
        return lax.optimization_barrier((value,) + others)[0]

    tags = jnp.concatenate(
        [
            (split_neuron >> 7).astype(BF)[None],
            (split_neuron & 127).astype(BF)[None],
            split_sign.astype(BF)[None],
            split_beta.T,
            jnp.zeros((TAGS - 5, slots), BF),
        ],
        axis=0,
    )
    top_rows = 3 * cap + TAGS
    top_spec = pl.BlockSpec((groups, top_rows, tile), lambda i: (0, 0, i))
    packed_top = pl.pallas_call(
        functools.partial(top_pack_kernel, groups, cap),
        grid=grid,
        in_specs=[
            smem,
            whole(TAGS, slots),
            plane_spec(1, slots),
            plane_spec(1, slots),
            pair_spec(1, slots),
            spec_spec,
        ],
        out_specs=top_spec,
        out_shape=jax.ShapeDtypeStruct((groups, top_rows, narrow), BF),
        scratch_shapes=[pltpu.VMEM((places, slots), BF)],
        compiler_params=params,
    )(counts, tags, state_lower, state_gap, state_alpha, spec)
    in_top = lax.all_to_all(packed_top, "dom", split_axis=0, concat_axis=0, tiled=True)

    half, quarter = groups // 2, groups // 8
    far = [list(range(half + i * quarter, half + (i + 1) * quarter)) for i in range(4)]
    mid = list(range(near, half))
    stages = [
        far[0] + mid[: len(mid) // 2],
        far[1] + far[3] + list(range(1, near)),
        far[2] + mid[len(mid) // 2 :],
    ]
    pool = pl.pallas_call(
        functools.partial(pool_pack_kernel, groups, cap),
        grid=grid,
        in_specs=[
            smem,
            plane_spec(0, slots),
            plane_spec(0, slots),
            pair_spec(0, slots),
            pair_spec(1, slots),
            spec_spec,
        ],
        out_specs=[part_spec(PLANES)] * groups,
        out_shape=[jax.ShapeDtypeStruct((PLANES, cap, narrow), BF)] * groups,
        scratch_shapes=[pltpu.VMEM((places, slots), BF)],
        compiler_params=params,
    )(counts, state_lower, state_gap, state_alpha, state_alpha, spec)

    panel = after(weight, in_top, pool[0])
    near_panels = []
    step = 1
    while step < near:
        other = swap(panel, step)
        near_panels.append(other)
        low_side = (device_pos & step) == 0
        panel = jnp.concatenate(
            [jnp.where(low_side, panel, other), jnp.where(low_side, other, panel)], axis=1
        )
        step *= 2

    in_top, pool = lax.optimization_barrier((in_top, pool))
    moved_lower, moved_gap, used_top, relaxed_top, moved_tags, offset = pl.pallas_call(
        functools.partial(top_kernel, groups, cap),
        grid=grid,
        in_specs=[smem, top_spec, spec_spec],
        out_specs=[
            plane_spec(1, rows),
            plane_spec(1, rows),
            flat_spec,
            both_spec,
            whole(rows, TAGS),
            whole(rows, 2),
        ],
        out_shape=[
            jax.ShapeDtypeStruct((2, rows, narrow), BF),
            jax.ShapeDtypeStruct((2, rows, narrow), BF),
            jax.ShapeDtypeStruct((rows, narrow), BF),
            jax.ShapeDtypeStruct((2, rows, narrow), BF),
            jax.ShapeDtypeStruct((rows, TAGS), F32),
            jax.ShapeDtypeStruct((rows, 2), F32),
        ],
        scratch_shapes=[pltpu.VMEM((rows, places), BF)],
        compiler_params=params,
    )(counts, in_top, spec)

    arrived = {0: pool[0]}

    def send_pool(stage, ready, *others):
        for k in stages[stage]:
            arrived[k] = swap(after(pool[k], *others), k)
        return after(ready, *[arrived[k] for k in stages[stage]])

    held = {0: relaxed_top.reshape(2 * rows, narrow)}
    for b in reversed(range(bits)):
        for delta in [d for d in held if d | (1 << b) not in held]:
            held[delta | (1 << b)] = swap(held[delta], near << b)
        if b == bits - 1:
            held[1 << b] = send_pool(0, held[1 << b], in_top)
            if bits > 1:
                held[1] = swap(held[0], near)
                held[1 << b] = after(held[1 << b], held[1], *near_panels)
    held[cores - 1] = send_pool(1, held[cores - 1], held[cores // 2])

    route = []
    for o in range(cores):
        for x in range(near):
            for c in range(cores):
                to = o ^ bit_reverse(c, bits)
                route.append(((o * near + x) * cores + c, (to * near + x) * cores + o))

    def product(rows_in):
        return lax.optimization_barrier(dot(rows_in, panel).astype(BF))

    def add(a, b):
        return (a.astype(F32) + b.astype(F32)).astype(BF)

    behind = [arrived[k] for k in range(1, near)]
    sums = [product(after(held[d], *behind)) for d in range(cores)]
    for b in range(bits):
        low_side = ((core_pos >> b) & 1) == 0
        count = len(sums) // 2
        folded = []
        for first, second in zip(sums[:count], sums[count:]):
            give = jnp.where(low_side, second, first)
            taken = swap_core(give, 1 << b)
            if b == bits - 1:
                taken = send_pool(2, taken, give)
            folded.append(add(jnp.where(low_side, first, second), taken))
        sums = folded
    coeff_low = lax.ppermute(sums[0], ("dom", "neu"), route)

    hbm = pl.BlockSpec(memory_space=pl.ANY)
    parts = [arrived[k] for k in range(groups)]
    moved_lower, moved_gap, moved_alpha = pl.pallas_call(
        functools.partial(settle_kernel, groups, cap),
        grid=grid,
        in_specs=[smem] + [part_spec(LOW_PLANES)] * groups + [hbm, hbm],
        out_specs=[plane_spec(0, rows), plane_spec(0, rows), pair_spec(0, rows)],
        out_shape=[
            jax.ShapeDtypeStruct((2, rows, narrow), BF),
            jax.ShapeDtypeStruct((2, rows, narrow), BF),
            jax.ShapeDtypeStruct((2, rows, 2, narrow), BF),
        ],
        input_output_aliases={groups + 1: 0, groups + 2: 1},
        scratch_shapes=[pltpu.VMEM((rows, places), BF)],
        compiler_params=params,
    )(counts, *parts, moved_lower, moved_gap)

    rest_spec = pl.BlockSpec((1, cap, tile), lambda i: (LOW_PLANES, 0, i))
    moved_alpha = pl.pallas_call(
        functools.partial(rest_kernel, groups, cap),
        grid=grid,
        in_specs=[smem] + [rest_spec] * groups + [flat_spec, spec_spec, hbm],
        out_specs=pair_spec(1, rows),
        out_shape=jax.ShapeDtypeStruct((2, rows, 2, narrow), BF),
        input_output_aliases={groups + 3: 0},
        scratch_shapes=[pltpu.VMEM((rows, places), BF)],
        compiler_params=params,
    )(counts, *parts, used_top, spec, moved_alpha)

    offset = pl.pallas_call(
        low_kernel,
        grid=grid,
        in_specs=[
            both_spec,
            whole(rows, TAGS),
            whole(rows, 2),
            plane_spec(0, rows),
            plane_spec(0, rows),
            pair_spec(0, rows),
        ],
        out_specs=whole(rows, 2),
        out_shape=jax.ShapeDtypeStruct((rows, 2), F32),
        compiler_params=params,
    )(
        coeff_low.reshape(2, rows, narrow),
        moved_tags,
        offset,
        moved_lower,
        moved_gap,
        moved_alpha,
    )

    terms = [offset] + [swap_core(offset, c) for c in range(1, cores)]
    while len(terms) > 1:
        terms = [a + b for a, b in zip(terms[0::2], terms[1::2])]
    totals = terms[0]
    bounds = jnp.stack([totals[:, 0], -totals[:, 1]], axis=1)
    neuron_ids = moved_tags[:, 0].astype(I32) * 128 + moved_tags[:, 1].astype(I32)
    sign_ids = moved_tags[:, 2].astype(I32)
    moved_beta = moved_tags[:, 3:5].astype(BF)
    return (moved_lower, moved_gap, moved_alpha, moved_beta, neuron_ids, sign_ids, bounds)


def solution(mesh):
    in_specs = (
        P(None, "dom", "neu"),
        P(None, "dom", "neu"),
        P(None, "dom", None, "neu"),
        P("dom", None),
        P("dom"),
        P("dom"),
        P(),
        P("neu"),
        P("neu", "dom"),
    )
    out_specs = (
        P(None, "dom", "neu"),
        P(None, "dom", "neu"),
        P(None, "dom", None, "neu"),
        P("dom", None),
        P("dom"),
        P("dom"),
        P("dom", None),
    )
    return jax.shard_map(shards, mesh=mesh, in_specs=in_specs, out_specs=out_specs, check_vma=False)
```

```python
import functools

import jax
import jax.numpy as jnp
from jax import lax
from jax.experimental import pallas as pl
from jax.experimental.pallas import tpu as pltpu
from jax.sharding import PartitionSpec as P

BF = jnp.bfloat16
F32 = jnp.float32
I32 = jnp.int32
TAGS = 8
LANES = 128
LOW_PLANES = 4
PLANES = 5
VMEM_BYTES = 48 << 20


def bit_reverse(value, bits):
    out = 0
    for b in range(bits):
        out |= ((value >> b) & 1) << (bits - 1 - b)
    return out


def tile_of(narrow):
    return min(1024, narrow)


def dot(a, b):
    return jnp.dot(a, b, preferred_element_type=F32)


def dot_nt(a, b):
    return lax.dot_general(a, b, (((1,), (1,)), ((), ())), preferred_element_type=F32)


def spread(values, index, cap):
    out = jnp.zeros(index.shape, I32)
    for k, value in enumerate(values):
        inside = (index >= k * cap) & (index < (k + 1) * cap)
        out = jnp.where(inside, value, out)
    return out


def prefix(counts_ref, row, end, groups):
    total = jnp.int32(0)
    for e in range(groups - 1):
        total = total + jnp.where(e < end, counts_ref[row, e], 0)
    return total


def column_prefix(counts_ref, column, end, groups):
    total = jnp.int32(0)
    for d in range(groups - 1):
        total = total + jnp.where(d < end, counts_ref[d, column], 0)
    return total


def partners(swapped, groups):
    me = lax.axis_index("dom")
    return [me ^ k if swapped else k for k in range(groups)]


def send_matrix(counts_ref, swapped, groups, cap, slots):
    me = lax.axis_index("dom")
    other = partners(swapped, groups)
    places = groups * cap
    place = lax.broadcasted_iota(I32, (places, 1), 0)
    shift = [prefix(counts_ref, me, other[k], groups) - k * cap for k in range(groups)]
    slot = lax.broadcasted_iota(I32, (places, slots), 1)
    return (slot == place + spread(shift, place, cap)).astype(BF)


def settle_matrix(counts_ref, swapped, groups, cap, rows):
    me = lax.axis_index("dom")
    places = groups * cap
    place = lax.broadcasted_iota(I32, (1, places), 1)
    shift, limit = [], []
    for k, partner in enumerate(partners(swapped, groups)):
        shift.append(column_prefix(counts_ref, me, partner, groups) - k * cap)
        limit.append(counts_ref[partner, me] + k * cap)
    target = jnp.where(place < spread(limit, place, cap), place + spread(shift, place, cap), -1)
    row = lax.broadcasted_iota(I32, (rows, places), 0)
    return (row == target).astype(BF)


def pool_pack_kernel(groups, cap, counts_ref, *refs):
    sources, out_refs, mat_ref = refs[: -groups - 1], refs[-groups - 1 : -1], refs[-1]
    slots = mat_ref.shape[1]

    @pl.when(pl.program_id(0) == 0)
    def _():
        mat_ref[...] = send_matrix(counts_ref, True, groups, cap, slots)

    mat = mat_ref[...]
    for p, plane in enumerate(pool_planes(*sources)):
        packed = dot(mat, plane).reshape(groups, cap, plane.shape[1]).astype(BF)
        for k in range(groups):
            out_refs[k][p] = packed[k]


def top_pack_kernel(groups, cap, counts_ref, neuron_ref, sign_ref, beta_ref, *refs):
    sources, out_ref, mat_ref = refs[:-2], refs[-2], refs[-1]
    slots = mat_ref.shape[1]

    @pl.when(pl.program_id(0) == 0)
    def _():
        mat_ref[...] = send_matrix(counts_ref, False, groups, cap, slots)
        me = lax.axis_index("dom")
        neuron, beta = neuron_ref[...], beta_ref[...].astype(F32)
        facts = [
            (neuron >> 7).astype(F32),
            (neuron & 127).astype(F32),
            sign_ref[...].astype(F32),
            beta[0:1],
            beta[1:2],
        ]
        line = lax.broadcasted_iota(I32, (TAGS, slots), 0)
        tags = jnp.zeros((TAGS, slots), F32)
        for t, fact in enumerate(facts):
            tags = jnp.where(line == t, fact, tags)
        tags = tags.astype(BF)
        place = lax.broadcasted_iota(I32, (LANES, slots), 0)
        slot = lax.broadcasted_iota(I32, (LANES, slots), 1)
        for e in range(groups):
            hit = (slot == place + prefix(counts_ref, me, e, groups)).astype(BF)
            out_ref[e, 3 * cap :, 0:LANES] = dot_nt(tags, hit).astype(BF)

    mat = mat_ref[...]
    for p, plane in enumerate(top_planes(*sources)):
        packed = dot(mat, plane).reshape(groups, cap, plane.shape[1])
        out_ref[:, p * cap : (p + 1) * cap] = packed.astype(BF)


def either(spec_ref, first, second):
    side = spec_ref[...].astype(F32) >= 0.0
    return jnp.where(side, first.astype(F32), second.astype(F32)).astype(BF)


def used_alpha(alpha_ref, spec_ref):
    return either(spec_ref, alpha_ref[0, :, 0, :], alpha_ref[0, :, 1, :])


def unused_alpha(alpha_ref, spec_ref):
    return either(spec_ref, alpha_ref[0, :, 1, :], alpha_ref[0, :, 0, :])


def top_planes(lower_ref, gap_ref, alpha_ref, spec_ref):
    return [lower_ref[0], gap_ref[0], used_alpha(alpha_ref, spec_ref)]


def pool_planes(lower_ref, gap_ref, alpha_ref, top_alpha_ref, spec_ref):
    return [
        lower_ref[0],
        gap_ref[0],
        alpha_ref[0, :, 0, :],
        alpha_ref[0, :, 1, :],
        unused_alpha(top_alpha_ref, spec_ref),
    ]


def slopes(low, gap, chosen, split_slope):
    high = low + gap
    active = low >= 0.0
    inactive = high <= 0.0
    ratio = high / gap
    upper_slope = jnp.where(active, 1.0, jnp.where(inactive, 0.0, ratio))
    intercept = jnp.where(active | inactive | chosen, 0.0, -ratio * low)
    upper_slope = jnp.where(chosen, split_slope, upper_slope)
    return high, active, inactive, upper_slope, intercept


def lower_slope_of(alpha, active, inactive, chosen, split_slope):
    slope = jnp.where(active, 1.0, jnp.where(inactive, 0.0, alpha))
    return jnp.where(chosen, split_slope, slope)


def row_facts(tags):
    neuron = tags[:, 0:1] * 128.0 + tags[:, 1:2]
    active_branch = tags[:, 2:3]
    split_slope = jnp.where(active_branch == 1.0, 1.0, 0.0)
    penalty = [tags[:, 3 + s : 4 + s] * (2.0 * active_branch - 1.0) for s in range(2)]
    return neuron.astype(I32), split_slope, penalty


def stacked(in_refs, plane):
    return jnp.concatenate([ref[plane] for ref in in_refs], axis=0)


def top_kernel(groups, cap, counts_ref, in_ref, spec_ref, *refs):
    lower_ref, gap_ref, used_ref, relaxed_ref, moved_ref, offset_ref, mat_ref = refs
    rows, tile = used_ref.shape
    step = pl.program_id(0)
    narrow = tile * pl.num_programs(0)

    @pl.when(step == 0)
    def _():
        mat_ref[...] = settle_matrix(counts_ref, False, groups, cap, rows)
        me = lax.axis_index("dom")
        row = lax.broadcasted_iota(I32, (rows, LANES), 0)
        place = lax.broadcasted_iota(I32, (rows, LANES), 1)
        moved = jnp.zeros((rows, TAGS), F32)
        for d in range(groups):
            first = column_prefix(counts_ref, me, d, groups)
            hit = ((row - place == first) & (place < counts_ref[d, me])).astype(BF)
            moved = moved + dot_nt(hit, in_ref[d, 3 * cap :, 0:LANES])
        moved_ref[...] = moved
        offset_ref[...] = jnp.zeros_like(offset_ref)

    mat = mat_ref[...]
    low, gap, used = (
        dot(mat, in_ref[:, p * cap : (p + 1) * cap].reshape(groups * cap, tile)) for p in range(3)
    )
    lower_ref[0] = low.astype(BF)
    gap_ref[0] = gap.astype(BF)
    used_ref[...] = used.astype(BF)
    neuron, split_slope, penalty = row_facts(moved_ref[...])
    base = (lax.axis_index("neu") + lax.axis_size("neu")) * narrow + step * tile
    chosen = neuron == base + lax.broadcasted_iota(I32, (rows, tile), 1)
    high, active, inactive, upper_slope, intercept = slopes(low, gap, chosen, split_slope)
    lower_slope = lower_slope_of(used, active, inactive, chosen, split_slope)
    spec = spec_ref[...].astype(F32)
    sums = []
    for s in range(2):
        coeff = spec if s == 0 else -spec
        negative = jnp.minimum(coeff, 0.0)
        value = jnp.maximum(coeff, 0.0) * lower_slope + negative * upper_slope
        value = value - jnp.where(chosen, penalty[s], 0.0)
        relaxed_ref[s] = value.astype(BF)
        sums.append(jnp.sum(negative * intercept, axis=1, keepdims=True))
    offset_ref[...] += jnp.concatenate(sums, axis=1)


def settle_kernel(groups, cap, counts_ref, *refs):
    in_refs, refs = refs[:groups], refs[groups:]
    _, _, lower_ref, gap_ref, alpha_ref, mat_ref = refs
    rows = mat_ref.shape[0]

    @pl.when(pl.program_id(0) == 0)
    def _():
        mat_ref[...] = settle_matrix(counts_ref, True, groups, cap, rows)

    mat = mat_ref[...]
    low, gap, *alpha = (
        dot(mat, stacked(in_refs, p)).astype(BF) for p in range(LOW_PLANES)
    )
    lower_ref[0] = low
    gap_ref[0] = gap
    for s in range(2):
        alpha_ref[0, :, s, :] = alpha[s]


def rest_kernel(groups, cap, counts_ref, *refs):
    in_refs, (used_ref, spec_ref, _, alpha_ref, mat_ref) = refs[:groups], refs[groups:]
    rows = mat_ref.shape[0]

    @pl.when(pl.program_id(0) == 0)
    def _():
        mat_ref[...] = settle_matrix(counts_ref, True, groups, cap, rows)

    rest = dot(mat_ref[...], stacked(in_refs, 0)).astype(BF)
    used = used_ref[...]
    alpha_ref[0, :, 0, :] = either(spec_ref, used, rest)
    alpha_ref[0, :, 1, :] = either(spec_ref, rest, used)


def low_kernel(
    first_ref, second_ref, tags_ref, before_ref, lower_ref, gap_ref, alpha_ref, offset_ref
):
    rows, tile = lower_ref.shape[1:]
    step = pl.program_id(0)
    narrow = tile * pl.num_programs(0)

    @pl.when(step == 0)
    def _():
        offset_ref[...] = before_ref[...]

    low = lower_ref[0].astype(F32)
    gap = gap_ref[0].astype(F32)
    neuron, split_slope, penalty = row_facts(tags_ref[...])
    base = lax.axis_index("neu") * narrow + step * tile
    chosen = neuron == base + lax.broadcasted_iota(I32, (rows, tile), 1)
    high, active, inactive, upper_slope, intercept = slopes(low, gap, chosen, split_slope)
    sums = []
    for s in range(2):
        alpha = alpha_ref[0, :, s, :].astype(F32)
        coeff = (first_ref, second_ref)[s][...].astype(F32)
        lower_slope = lower_slope_of(alpha, active, inactive, chosen, split_slope)
        negative = jnp.minimum(coeff, 0.0)
        value = jnp.maximum(coeff, 0.0) * lower_slope + negative * upper_slope
        value = value - jnp.where(chosen, penalty[s], 0.0)
        term = negative * intercept + jnp.maximum(value, 0.0) * low + jnp.minimum(value, 0.0) * high
        sums.append(jnp.sum(term, axis=1, keepdims=True))
    offset_ref[...] += jnp.concatenate(sums, axis=1)


def shards(
    state_lower,
    state_gap,
    state_alpha,
    split_beta,
    split_neuron,
    split_sign,
    send_counts,
    spec_row,
    weight,
):
    groups = lax.axis_size("dom")
    cores = lax.axis_size("neu")
    near = groups // cores
    bits = cores.bit_length() - 1
    assert near * cores == groups and 1 << bits == cores
    device_pos = lax.axis_index("dom")
    core_pos = lax.axis_index("neu")
    slots = state_lower.shape[1]
    rows = slots // 2
    cap = slots // groups
    places = groups * cap
    narrow = state_lower.shape[2]
    tile = tile_of(narrow)
    grid = (narrow // tile,)
    counts = send_counts.astype(I32)
    spec = spec_row[None, :]
    params = pltpu.CompilerParams(vmem_limit_bytes=VMEM_BYTES)

    smem = pl.BlockSpec(memory_space=pltpu.SMEM)

    def plane_spec(layer, count):
        return pl.BlockSpec((1, count, tile), lambda i: (layer, 0, i))

    def pair_spec(layer, count):
        return pl.BlockSpec((1, count, 2, tile), lambda i: (layer, 0, 0, i))

    def part_spec(planes):
        return pl.BlockSpec((planes, cap, tile), lambda i: (0, 0, i))

    def whole(*shape):
        return pl.BlockSpec(shape, lambda i: (0,) * len(shape))

    spec_spec = pl.BlockSpec((1, tile), lambda i: (0, i))
    flat_spec = pl.BlockSpec((rows, tile), lambda i: (0, i))
    both_spec = pl.BlockSpec((2, rows, tile), lambda i: (0, 0, i))

    def swap(value, mask):
        return lax.ppermute(value, "dom", [(d, d ^ mask) for d in range(groups)])

    def swap_core(value, mask):
        return lax.ppermute(value, "neu", [(c, c ^ mask) for c in range(cores)])

    def after(value, *others):
        return lax.optimization_barrier((value,) + others)[0]

    top_rows = 3 * cap + TAGS
    top_spec = pl.BlockSpec((groups, top_rows, tile), lambda i: (0, 0, i))
    packed_top = pl.pallas_call(
        functools.partial(top_pack_kernel, groups, cap),
        grid=grid,
        in_specs=[
            smem,
            whole(1, slots),
            whole(1, slots),
            whole(2, slots),
            plane_spec(1, slots),
            plane_spec(1, slots),
            pair_spec(1, slots),
            spec_spec,
        ],
        out_specs=top_spec,
        out_shape=jax.ShapeDtypeStruct((groups, top_rows, narrow), BF),
        scratch_shapes=[pltpu.VMEM((places, slots), BF)],
        compiler_params=params,
    )(
        counts,
        split_neuron[None],
        split_sign[None],
        split_beta.T,
        state_lower,
        state_gap,
        state_alpha,
        spec,
    )
    in_top = lax.all_to_all(packed_top, "dom", split_axis=0, concat_axis=0, tiled=True)

    half, quarter = groups // 2, groups // 8
    far = [list(range(half + i * quarter, half + (i + 1) * quarter)) for i in range(4)]
    mid = list(range(near, half))
    stages = [
        far[0] + mid[: len(mid) // 2],
        far[1] + far[3] + list(range(1, near)),
        far[2] + mid[len(mid) // 2 :],
    ]
    pool = pl.pallas_call(
        functools.partial(pool_pack_kernel, groups, cap),
        grid=grid,
        in_specs=[
            smem,
            plane_spec(0, slots),
            plane_spec(0, slots),
            pair_spec(0, slots),
            pair_spec(1, slots),
            spec_spec,
        ],
        out_specs=[part_spec(PLANES)] * groups,
        out_shape=[jax.ShapeDtypeStruct((PLANES, cap, narrow), BF)] * groups,
        scratch_shapes=[pltpu.VMEM((places, slots), BF)],
        compiler_params=params,
    )(counts, state_lower, state_gap, state_alpha, state_alpha, spec)

    panel = after(weight, in_top, pool[0])
    near_panels = []
    step = 1
    while step < near:
        other = swap(panel, step)
        near_panels.append(other)
        low_side = (device_pos & step) == 0
        panel = jnp.concatenate(
            [jnp.where(low_side, panel, other), jnp.where(low_side, other, panel)], axis=1
        )
        step *= 2

    in_top, pool = lax.optimization_barrier((in_top, pool))
    moved_lower, moved_gap, used_top, relaxed_top, moved_tags, offset = pl.pallas_call(
        functools.partial(top_kernel, groups, cap),
        grid=grid,
        in_specs=[smem, top_spec, spec_spec],
        out_specs=[
            plane_spec(1, rows),
            plane_spec(1, rows),
            flat_spec,
            both_spec,
            whole(rows, TAGS),
            whole(rows, 2),
        ],
        out_shape=[
            jax.ShapeDtypeStruct((2, rows, narrow), BF),
            jax.ShapeDtypeStruct((2, rows, narrow), BF),
            jax.ShapeDtypeStruct((rows, narrow), BF),
            jax.ShapeDtypeStruct((2, rows, narrow), BF),
            jax.ShapeDtypeStruct((rows, TAGS), F32),
            jax.ShapeDtypeStruct((rows, 2), F32),
        ],
        scratch_shapes=[pltpu.VMEM((rows, places), BF)],
        compiler_params=params,
    )(counts, in_top, spec)

    arrived = {0: pool[0]}

    def send_pool(stage, ready, *others):
        for k in stages[stage]:
            arrived[k] = swap(after(pool[k], *others), k)
        return after(ready, *[arrived[k] for k in stages[stage]])

    held = {0: relaxed_top.reshape(2 * rows, narrow)}
    for b in reversed(range(bits)):
        for delta in [d for d in held if d | (1 << b) not in held]:
            held[delta | (1 << b)] = swap(held[delta], near << b)
        if b == bits - 1:
            held[1 << b] = send_pool(0, held[1 << b], in_top)
            if bits > 1:
                held[1] = swap(held[0], near)
                held[1 << b] = after(held[1 << b], held[1], *near_panels)
    held[cores - 1] = send_pool(1, held[cores - 1], held[cores // 2])

    route = []
    for o in range(cores):
        for x in range(near):
            for c in range(cores):
                to = o ^ bit_reverse(c, bits)
                route.append(((o * near + x) * cores + c, (to * near + x) * cores + o))

    def product(rows_in):
        return lax.optimization_barrier(dot(rows_in, panel).astype(BF))

    def add(a, b):
        return (a.astype(F32) + b.astype(F32)).astype(BF)

    behind = [arrived[k] for k in range(1, near)]
    sums = [product(after(held[d], *behind)) for d in range(cores)]
    for b in range(bits - 1):
        low_side = ((core_pos >> b) & 1) == 0
        count = len(sums) // 2
        folded = []
        for first, second in zip(sums[:count], sums[count:]):
            taken = swap_core(jnp.where(low_side, second, first), 1 << b)
            folded.append(add(jnp.where(low_side, first, second), taken))
        sums = [lax.optimization_barrier(value) for value in folded[:-1]] + folded[-1:]

    low_side = ((core_pos >> (bits - 1)) & 1) == 0
    gives = jnp.where(low_side, sums[1], sums[0])
    keeps = jnp.where(low_side, sums[0], sums[1])
    coeff = []
    taken = gives
    for s in range(2):
        half_rows = slice(s * rows, (s + 1) * rows)
        taken = swap_core(after(gives[half_rows], taken), 1 << (bits - 1))
        if s == 1:
            taken = send_pool(2, taken, gives)
        value = add(keeps[half_rows], taken)
        coeff.append(lax.ppermute(value, ("dom", "neu"), route))

    hbm = pl.BlockSpec(memory_space=pl.ANY)
    parts = [arrived[k] for k in range(groups)]
    moved_lower, moved_gap, moved_alpha = pl.pallas_call(
        functools.partial(settle_kernel, groups, cap),
        grid=grid,
        in_specs=[smem] + [part_spec(LOW_PLANES)] * groups + [hbm, hbm],
        out_specs=[plane_spec(0, rows), plane_spec(0, rows), pair_spec(0, rows)],
        out_shape=[
            jax.ShapeDtypeStruct((2, rows, narrow), BF),
            jax.ShapeDtypeStruct((2, rows, narrow), BF),
            jax.ShapeDtypeStruct((2, rows, 2, narrow), BF),
        ],
        input_output_aliases={groups + 1: 0, groups + 2: 1},
        scratch_shapes=[pltpu.VMEM((rows, places), BF)],
        compiler_params=params,
    )(counts, *parts, moved_lower, moved_gap)

    rest_spec = pl.BlockSpec((1, cap, tile), lambda i: (LOW_PLANES, 0, i))
    moved_alpha = pl.pallas_call(
        functools.partial(rest_kernel, groups, cap),
        grid=grid,
        in_specs=[smem] + [rest_spec] * groups + [flat_spec, spec_spec, hbm],
        out_specs=pair_spec(1, rows),
        out_shape=jax.ShapeDtypeStruct((2, rows, 2, narrow), BF),
        input_output_aliases={groups + 3: 0},
        scratch_shapes=[pltpu.VMEM((rows, places), BF)],
        compiler_params=params,
    )(counts, *parts, used_top, spec, moved_alpha)

    offset = pl.pallas_call(
        low_kernel,
        grid=grid,
        in_specs=[
            flat_spec,
            flat_spec,
            whole(rows, TAGS),
            whole(rows, 2),
            plane_spec(0, rows),
            plane_spec(0, rows),
            pair_spec(0, rows),
        ],
        out_specs=whole(rows, 2),
        out_shape=jax.ShapeDtypeStruct((rows, 2), F32),
        compiler_params=params,
    )(
        *coeff,
        moved_tags,
        offset,
        moved_lower,
        moved_gap,
        moved_alpha,
    )

    terms = [offset] + [swap_core(offset, c) for c in range(1, cores)]
    while len(terms) > 1:
        terms = [a + b for a, b in zip(terms[0::2], terms[1::2])]
    totals = terms[0]
    bounds = totals * jnp.array([1.0, -1.0], dtype=F32)
    neuron_ids = moved_tags[:, 0].astype(I32) * 128 + moved_tags[:, 1].astype(I32)
    sign_ids = moved_tags[:, 2].astype(I32)
    moved_beta = moved_tags[:, 3:5].astype(BF)
    return (moved_lower, moved_gap, moved_alpha, moved_beta, neuron_ids, sign_ids, bounds)


def solution(mesh):
    in_specs = (
        P(None, "dom", "neu"),
        P(None, "dom", "neu"),
        P(None, "dom", None, "neu"),
        P("dom", None),
        P("dom"),
        P("dom"),
        P(),
        P("neu"),
        P("neu", "dom"),
    )
    out_specs = (
        P(None, "dom", "neu"),
        P(None, "dom", "neu"),
        P(None, "dom", None, "neu"),
        P("dom", None),
        P("dom"),
        P("dom"),
        P("dom", None),
    )
    return jax.shard_map(shards, mesh=mesh, in_specs=in_specs, out_specs=out_specs, check_vma=False)
```
